32 devices in a mesh: dp: 2 (over core), pipe: 2 (over x), ctx: 8 (over z, y).
Axes of the slice: x: 2, y: 2, z: 4, core: 2. Of those that a mesh axis runs over, the one named last changes fastest.
Arguments:
- queries: bfloat16 [4, 1024, 2048], P(('dp', 'pipe'), 'ctx'), parts along dimension 0, may hold values from -6 to 6
- section_key_state: bfloat16 [4, 1024, 256], P(('dp', 'pipe'), 'ctx'), parts along dimension 0, may hold values from -6 to 6
- section_value_state: bfloat16 [4, 1024, 256], P(('dp', 'pipe'), 'ctx'), parts along dimension 0, may hold values from -6 to 6
- out_grad: bfloat16 [4, 1024, 2048], P(('dp', 'pipe'), 'ctx'), parts along dimension 0, may hold values from -6 to 6
- doc_blocks: int32 [4, 4], P(('dp', 'pipe')), parts along dimension 0, may hold values from 1 to 4, 8 in all within a row
Outputs:
- attention: bfloat16 [4, 1024, 2048], P(('dp', 'pipe'), 'ctx'), parts along dimension 0
- query_grads: bfloat16 [4, 1024, 2048], P(('dp', 'pipe'), 'ctx'), parts along dimension 0
- key_grads: bfloat16 [4, 1024, 256], P(('dp', 'pipe'), 'ctx'), parts along dimension 0
- value_grads: bfloat16 [4, 1024, 256], P(('dp', 'pipe'), 'ctx'), parts along dimension 0
The draws below stay inside these ranges and needn't reach their ends.
There are 2 independent parts, one for each index of `dp`. The reference program is written for one: setup_inputs(seed, part) draws one part's arguments, and reference() takes and returns one part's arrays. A program takes and returns all parts, laid end to end along the dimension named above; each array names one. Nothing has to cross between parts.
Inputs may be any that keep to these rules, and one draw needn't show every extreme that they name: `doc_blocks`: each row sums to 8, and one document of each row has exactly 4 blocks.
All inputs are finite; a program needn't handle non-finite values.
Results may differ from the reference program's by a relative error of at most 0.012.
The reference program's roundings to bfloat16 on the way count: a program that leaves them out, or rounds other values in their place, can miss the bound.
Values may be sent and summed in bfloat16 or wider, within the bound.
A program may use at most 64 MiB of HBM per device.

```python
import math
import jax
import jax.numpy as jnp
import numpy as np
from jax import lax

QUERY_HEAD_COUNT = 16
KEY_VALUE_HEADS = 2
HEAD_SIZE = 128
BLK = 128
TOK_DEV = 128
RELAY_SECTIONS = 2
SECTION_TOKENS = 1024
BLOCKS = 8
NDOCS = 4
MOST = 4


def backdrop_mask(key, array_shape):
    return jnp.clip(jax.random.normal(key, array_shape, jnp.float32), -4.0, 4.0)


def draw_section_key_state(key, part):
    final_result = backdrop_mask(jax.random.fold_in(key, 5), (RELAY_SECTIONS, SECTION_TOKENS, KEY_VALUE_HEADS * HEAD_SIZE))
    return final_result.astype(jnp.bfloat16)


def draw_queries(key, part):
    final_result = backdrop_mask(jax.random.fold_in(key, 7), (RELAY_SECTIONS, SECTION_TOKENS, QUERY_HEAD_COUNT * HEAD_SIZE))
    return final_result.astype(jnp.bfloat16)


def block_scale(key, dims, split, least, top_value):
    gain, own = 1.0, jax.random.fold_in(key, 6)
    for axis_at, shards_of in split:
        steps = jnp.exp(jax.random.uniform(jax.random.fold_in(own, axis_at), (shards_of,), jnp.float32, least / len(split), top_value / len(split)))
        gain = gain * jnp.repeat(steps, dims[axis_at] // shards_of).reshape([-1 if axis == axis_at else 1 for axis in range(len(dims))])
    return gain


def profile(number_of, total, reach, slope):
    portions = [(1 << 20) // math.isqrt(standing ** slope) + 1 for standing in range(2, number_of + 1)]
    rest, given = total - reach - (number_of - 1), [1] * (number_of - 1)
    while rest > 0:
        free = [i for i in range(number_of - 1) if given[i] < reach]
        whole, budget = sum([portions[i] for i in free]), rest
        for i in free:
            addition = min(reach - given[i], max(1, budget * portions[i] // whole), rest)
            given[i] = given[i] + addition
            rest = rest - addition
    return np.array([reach] + given)


def uneven(stream_key, number_of, total, bound, lean):
    if number_of == 2:
        one = jax.random.randint(stream_key, (), max(1, total - bound), min(bound, total - 1) + 1)
        return jnp.stack([one, total - one])
    sizes = jnp.asarray(profile(number_of, total, bound, lean), jnp.int32)
    pairs = (number_of - 1) // 2
    giver, receiver = sizes[1:1 + 2 * pairs:2], sizes[2:2 + 2 * pairs:2]
    slack = jnp.minimum(giver - 1, bound - receiver)
    moved = jax.random.randint(jax.random.fold_in(stream_key, 1), (pairs,), 0, 1 << 20) % (slack + 1)
    sizes = sizes.at[1:1 + 2 * pairs:2].set(giver - moved).at[2:2 + 2 * pairs:2].set(receiver + moved)
    return sizes[jax.random.permutation(jax.random.fold_in(stream_key, 2), number_of)]


def scatter_about(own_key, dims, deviation, limit, cuts=(), kind=jnp.bfloat16):
    values = deviation * jax.random.normal(own_key, dims, jnp.float32)
    if cuts:
        values = values * block_scale(own_key, dims, cuts, -0.22, 0.18)
    return jnp.clip(values, -limit, limit).astype(kind)


def setup_inputs(seed: int = 0, part: int = 0) -> dict:
    key_list = jax.random.split(jax.random.key(seed), 6)
    own_keys = jax.random.split(jax.random.fold_in(key_list[5], part), 6)
    return {
        "queries": draw_queries(jax.random.fold_in(jax.random.fold_in(key_list[5], part), 71), part),
        "section_key_state": draw_section_key_state(jax.random.fold_in(jax.random.fold_in(key_list[5], part), 71), part),
        "section_value_state": scatter_about(own_keys[2], (RELAY_SECTIONS, SECTION_TOKENS, KEY_VALUE_HEADS * HEAD_SIZE), 1.0, 6.0, ((0, 2), (1, 8))),
        "out_grad": scatter_about(own_keys[3], (RELAY_SECTIONS, SECTION_TOKENS, QUERY_HEAD_COUNT * HEAD_SIZE), 1.0, 6.0, ((0, 2), (1, 8))),
        "doc_blocks": jax.vmap(lambda own: uneven(own, NDOCS, BLOCKS, MOST, 2))(jax.random.split(own_keys[4], RELAY_SECTIONS)).reshape((RELAY_SECTIONS, NDOCS)).astype(jnp.int32),
    }


def positions_of(shard_rows, shard_count):
    half_rows = shard_rows // 2
    device_at = jnp.arange(shard_count, dtype=jnp.int32)[:, None]
    offsets = jnp.arange(half_rows, dtype=jnp.int32)[None, :]
    lower_half = device_at * half_rows + offsets
    upper_half = (2 * shard_count - 1 - device_at) * half_rows + offsets
    return jnp.concatenate([lower_half, upper_half], axis=1).reshape(shard_rows * shard_count)

def one_section(section_inputs):
    queries, section_key_state, section_value_state, out_grad, doc_lengths = section_inputs
    group_width = QUERY_HEAD_COUNT // KEY_VALUE_HEADS
    shard_count = SECTION_TOKENS // TOK_DEV
    inverse_root = 1.0 / math.sqrt(HEAD_SIZE)
    positions = positions_of(TOK_DEV, shard_count)
    bounds = (jnp.cumsum(doc_lengths) * BLK)[:-1]
    documents = lax.optimization_barrier(jnp.sum((positions[:, None] >= bounds[None, :]).astype(jnp.int32), axis=1))
    visible = (documents[:, None] == documents[None, :]) & (positions[None, :] <= positions[:, None])
    query_heads = queries.reshape(SECTION_TOKENS, QUERY_HEAD_COUNT, HEAD_SIZE).transpose(1, 0, 2)
    grad_heads = out_grad.reshape(SECTION_TOKENS, QUERY_HEAD_COUNT, HEAD_SIZE).transpose(1, 0, 2)
    key_head_rows = section_key_state.reshape(SECTION_TOKENS, KEY_VALUE_HEADS, HEAD_SIZE).transpose(1, 0, 2)
    value_head_rows = section_value_state.reshape(SECTION_TOKENS, KEY_VALUE_HEADS, HEAD_SIZE).transpose(1, 0, 2)

    def per_head(carried, head_inputs):
        key_sum, value_sum = carried
        head_at, query_head, grad_head = head_inputs
        group_at = head_at // group_width
        key_head = key_head_rows[group_at]
        value_head = value_head_rows[group_at]
        scores = jnp.dot(query_head, key_head.T, preferred_element_type=jnp.float32) * inverse_root
        scores = jnp.where(visible, scores, -jnp.inf)
        row_max = lax.optimization_barrier(jnp.max(scores, axis=1, keepdims=True))
        log_total = row_max + jnp.log(lax.optimization_barrier(jnp.sum(jnp.exp(scores - row_max), axis=1, keepdims=True)))
        weights = jnp.exp(scores - log_total)
        weights_low = lax.optimization_barrier(weights.astype(jnp.bfloat16))
        head_out = jnp.dot(weights_low, value_head, preferred_element_type=jnp.float32).astype(jnp.bfloat16)
        head_out = lax.optimization_barrier(head_out)
        row_dot = lax.optimization_barrier(jnp.sum(grad_head.astype(jnp.float32) * head_out.astype(jnp.float32), axis=1, keepdims=True))
        weight_grad = jnp.dot(grad_head, value_head.T, preferred_element_type=jnp.float32)
        score_grad = (weights * (weight_grad - row_dot) * inverse_root).astype(jnp.bfloat16)
        score_grad = lax.optimization_barrier(score_grad)
        query_grad = jnp.dot(score_grad, key_head, preferred_element_type=jnp.float32).astype(jnp.bfloat16)
        score_dev = score_grad.astype(jnp.float32).reshape(shard_count, TOK_DEV, SECTION_TOKENS)
        weight_dev = weights_low.astype(jnp.float32).reshape(shard_count, TOK_DEV, SECTION_TOKENS)
        query_dev = query_head.astype(jnp.float32).reshape(shard_count, TOK_DEV, HEAD_SIZE)
        grad_dev = grad_head.astype(jnp.float32).reshape(shard_count, TOK_DEV, HEAD_SIZE)
        key_part = jnp.einsum('nts,ntd->nsd', score_dev, query_dev, precision=lax.Precision.HIGHEST)
        value_part = jnp.einsum('nts,ntd->nsd', weight_dev, grad_dev, precision=lax.Precision.HIGHEST)
        key_sum = key_sum.at[group_at].add(key_part)
        value_sum = value_sum.at[group_at].add(value_part)
        return ((key_sum, value_sum), (head_out, query_grad))
    blank_sum = jnp.zeros((KEY_VALUE_HEADS, shard_count, SECTION_TOKENS, HEAD_SIZE), jnp.float32)
    head_ids = jnp.arange(QUERY_HEAD_COUNT, dtype=jnp.int32)
    (key_sum, value_sum), (head_outs, query_grads) = lax.scan(per_head, (blank_sum, blank_sum), (head_ids, query_heads, grad_heads))
    key_low = lax.optimization_barrier(key_sum.astype(jnp.bfloat16))
    value_low = lax.optimization_barrier(value_sum.astype(jnp.bfloat16))
    key_gradient = lax.optimization_barrier(jnp.sum(key_low.astype(jnp.float32), axis=1)).astype(jnp.bfloat16)
    value_gradient = lax.optimization_barrier(jnp.sum(value_low.astype(jnp.float32), axis=1)).astype(jnp.bfloat16)
    attention = head_outs.transpose(1, 0, 2).reshape(SECTION_TOKENS, QUERY_HEAD_COUNT * HEAD_SIZE)
    query_flat = query_grads.transpose(1, 0, 2).reshape(SECTION_TOKENS, QUERY_HEAD_COUNT * HEAD_SIZE)
    flat_keys = key_gradient.transpose(1, 0, 2).reshape(SECTION_TOKENS, KEY_VALUE_HEADS * HEAD_SIZE)
    flat_values = value_gradient.transpose(1, 0, 2).reshape(SECTION_TOKENS, KEY_VALUE_HEADS * HEAD_SIZE)
    return (attention, query_flat, flat_keys, flat_values)

def earlier(stacked_values):
    return jnp.concatenate([stacked_values[1:], jnp.zeros_like(stacked_values[:1])], axis=0)

def reference(queries, section_key_state, section_value_state, out_grad, doc_blocks):
    attention, query_grad, key_gradient, value_gradient = lax.map(one_section, (queries, section_key_state, section_value_state, out_grad, doc_blocks))
    return (attention, earlier(query_grad), earlier(key_gradient), earlier(value_gradient))
```

```python
import functools
import math

import jax
import jax.numpy as jnp
from jax import lax
from jax.experimental import pallas as pl
from jax.experimental.pallas import tpu as pltpu
from jax.sharding import PartitionSpec as P

KEY_VALUE_HEADS = 2
HEAD_SIZE = 128
BLK = 128
LOG2E = math.log2(math.e)
F32 = jnp.float32
BF16 = jnp.bfloat16


def dot(a, b, contract):
    return lax.dot_general(a, b, (contract, ((), ())), preferred_element_type=F32)


def kernel(
    count, sections, heads, docs,
    doc_ref, q_ref, k_ref, v_ref, go_ref,
    att_ref, qg_ref, kg_ref, vg_ref,
    kv, acc, dkv, recv, probs, dq, fin,
    kv_send, kv_recv, part_send, part_recv, dq_send, dq_recv, fin_send, fin_recv,
):
    rows = q_ref.shape[1]
    half = rows // 2
    width = KEY_VALUE_HEADS * HEAD_SIZE
    group = heads // KEY_VALUE_HEADS
    lanes = group * half
    span = count * half
    scale = 1.0 / math.sqrt(HEAD_SIZE)
    me = lax.axis_index("ctx")
    section = lax.axis_index("pipe")
    has_grads = section > 0
    has_next = section < sections - 1

    def block_rows(block):
        return pl.ds(pl.multiple_of(block * half, half), half)

    def start_of(c):
        return 2 * ((2 * count - 1 - c) // 2) - count + 2

    def upper_of(d):
        return 2 * count - 1 - d

    def upper_used(c, d):
        return c <= d

    def lower_for_upper(c, d):
        return d >= start_of(c)

    def lower_used(c, d):
        return (d <= c) | (d >= start_of(c))

    kv[...] = jnp.zeros_like(kv)
    kv[block_rows(me), :width] = k_ref[0, :half, :]
    kv[block_rows(me), width:] = v_ref[0, :half, :]
    kv[block_rows(upper_of(me)), :width] = k_ref[0, half:, :]
    kv[block_rows(upper_of(me)), width:] = v_ref[0, half:, :]

    barrier = pltpu.get_barrier_semaphore()
    MESH = pl.DeviceIdType.MESH
    for step in range(1, count):
        pl.semaphore_signal(
            barrier, inc=1, device_id={"ctx": lax.rem(me + step, count)}, device_id_type=MESH
        )

    @pl.when(has_grads)
    def _():
        pl.semaphore_signal(barrier, inc=1, device_id={"pipe": section - 1}, device_id_type=MESH)

    @pl.when(has_next)
    def _():
        pl.semaphore_signal(barrier, inc=1, device_id={"pipe": section + 1}, device_id_type=MESH)

    pl.semaphore_wait(
        barrier, count - 1 + jnp.minimum(section, 1) + jnp.minimum(sections - 1 - section, 1)
    )

    def kv_copy(block, part, step_send, step_recv, target):
        return pltpu.make_async_remote_copy(
            src_ref=kv.at[block_rows(block)],
            dst_ref=kv.at[block_rows(block)],
            send_sem=kv_send.at[step_send, part],
            recv_sem=kv_recv.at[step_recv, part],
            device_id={"ctx": target},
            device_id_type=MESH,
        )

    for step in range(1, count):
        to = lax.rem(me + step, count)

        @pl.when(upper_used(to, me))
        def _():
            kv_copy(upper_of(me), 1, step, step, to).start()

        @pl.when(lower_used(to, me))
        def _():
            kv_copy(me, 0, step, step, to).start()

    acc[...] = jnp.zeros_like(acc)

    @pl.when(jnp.logical_not(has_next))
    def _():
        qg_ref[...] = jnp.zeros_like(qg_ref)
        kg_ref[...] = jnp.zeros_like(kg_ref)
        vg_ref[...] = jnp.zeros_like(vg_ref)

    def kv_wait(step, part, source, block):
        kv_copy(block, part, step, step, source).wait_recv()

    def stack(ref, part, g):
        return jnp.concatenate(
            [
                ref[0, part * half:(part + 1) * half, h * HEAD_SIZE:(h + 1) * HEAD_SIZE]
                for h in range(g * group, (g + 1) * group)
            ],
            axis=0,
        )

    def unstack(ref, part, g, value):
        for j in range(group):
            h = g * group + j
            ref[0, part * half:(part + 1) * half, h * HEAD_SIZE:(h + 1) * HEAD_SIZE] = value[
                j * half:(j + 1) * half
            ]

    def dq_copy(part, g):
        index = part * KEY_VALUE_HEADS + g
        cut = (
            slice(None),
            pl.ds(part * half, half),
            pl.ds(g * group * HEAD_SIZE, group * HEAD_SIZE),
        )
        return pltpu.make_async_remote_copy(
            src_ref=dq.at[cut],
            dst_ref=qg_ref.at[cut],
            send_sem=dq_send.at[index],
            recv_sem=dq_recv.at[index],
            device_id={"pipe": section - 1},
            device_id_type=MESH,
        )

    def unit(part, g):
        first = start_of(me) if part else 0
        own = upper_of(me) if part else me
        base = first * half
        window = pl.ds(pl.multiple_of(base, BLK), span) if part else pl.ds(0, span)
        key_cols = slice(g * HEAD_SIZE, (g + 1) * HEAD_SIZE)
        value_cols = slice(width + g * HEAD_SIZE, width + (g + 1) * HEAD_SIZE)
        query = stack(q_ref, part, g)
        grad = stack(go_ref, part, g)
        keys = kv[window, key_cols]
        values = kv[window, value_cols]
        bound = jnp.int32(0)
        low = jnp.int32(0)
        for j in range(docs - 1):
            bound = bound + doc_ref[0, j] * BLK
            low = jnp.where(bound <= own * half, bound, low)
        key_pos = base + lax.broadcasted_iota(jnp.int32, (span, lanes), 0)
        query_pos = own * half + lax.broadcasted_iota(jnp.int32, (span, lanes), 1) % half
        visible = (key_pos >= low) & (key_pos <= query_pos)
        scores = dot(keys, query, ((1,), (1,))) * (scale * LOG2E)
        scores = jnp.where(visible, scores, -jnp.inf)
        top = jnp.max(scores, axis=0, keepdims=True)
        weights = jnp.exp2(scores - top)
        weights = weights * (1.0 / jnp.sum(weights, axis=0, keepdims=True))
        probs[...] = weights
        low_weights = weights.astype(BF16)
        out = dot(values.T, low_weights, ((1,), (0,))).astype(BF16)
        unstack(att_ref, part, g, out.T)

        @pl.when(has_grads)
        def _():
            delta = jnp.sum(grad.T.astype(F32) * out.astype(F32), axis=0, keepdims=True)
            weight_grad = dot(values, grad, ((1,), (1,)))
            p = probs[...]
            score_grad = (p * (weight_grad - delta) * scale).astype(BF16)
            query_grad = dot(keys.T, score_grad, ((1,), (0,))).astype(BF16)
            unstack(dq, part, g, query_grad.T)
            dq_copy(part, g).start()
            acc[window, key_cols] += dot(score_grad, query, ((1,), (0,)))
            acc[window, value_cols] += dot(p.astype(BF16), grad, ((1,), (0,)))

    def part_copy(block, part, owner, step):
        return pltpu.make_async_remote_copy(
            src_ref=dkv.at[block_rows(block)],
            dst_ref=recv.at[step, part],
            send_sem=part_send.at[step, part],
            recv_sem=part_recv.at[step, part],
            device_id={"ctx": owner},
            device_id_type=MESH,
        )

    for step in range(1, count):
        source = lax.rem(me + count - step, count)

        @pl.when(upper_used(me, source))
        def _():
            kv_wait(step, 1, source, upper_of(source))

        @pl.when(lower_for_upper(me, source))
        def _():
            kv_wait(step, 0, source, source)

    for g in range(KEY_VALUE_HEADS):
        unit(1, g)

    @pl.when(has_grads)
    def _():
        dkv[span:, :] = acc[span:, :].astype(BF16)
        for step in range(1, count):
            owner = lax.rem(me + step, count)

            @pl.when(upper_used(me, owner))
            def _():
                part_copy(upper_of(owner), 1, owner, step).start()

    for step in range(1, count):
        source = lax.rem(me + count - step, count)

        @pl.when(lower_used(me, source) & jnp.logical_not(lower_for_upper(me, source)))
        def _():
            kv_wait(step, 0, source, source)

    for g in range(KEY_VALUE_HEADS):
        unit(0, g)

    @pl.when(has_grads)
    def _():
        dkv[:span, :] = acc[:span, :].astype(BF16)
        for step in range(1, count):
            owner = lax.rem(me + step, count)

            @pl.when(lower_used(me, owner))
            def _():
                part_copy(owner, 0, owner, step).start()

        def fin_copy(index):
            out = (kg_ref, vg_ref)[index]
            return pltpu.make_async_remote_copy(
                src_ref=fin.at[pl.ds(index, 1)],
                dst_ref=out,
                send_sem=fin_send.at[index],
                recv_sem=fin_recv.at[index],
                device_id={"pipe": section - 1},
                device_id_type=MESH,
            )

        for part in (1, 0):
            block = upper_of(me) if part else me
            used = upper_used if part else lower_used
            acc[:half, :] = dkv[block_rows(block), :].astype(F32)
            for step in range(1, count):
                source = lax.rem(me + count - step, count)

                @pl.when(used(source, me))
                def _():
                    part_copy(block, part, source, step).wait_recv()
                    acc[:half, :] += recv[step, part].astype(F32)

            total = acc[:half, :].astype(BF16)
            fin[0, part * half:(part + 1) * half, :] = total[:, :width]
            fin[1, part * half:(part + 1) * half, :] = total[:, width:]
        for index in range(2):
            fin_copy(index).start()
        for step in range(1, count):
            owner = lax.rem(me + step, count)

            @pl.when(upper_used(me, owner))
            def _():
                part_copy(upper_of(owner), 1, owner, step).wait_send()

            @pl.when(lower_used(me, owner))
            def _():
                part_copy(owner, 0, owner, step).wait_send()

        for part in (1, 0):
            for g in range(KEY_VALUE_HEADS):
                dq_copy(part, g).wait_send()
        for index in range(2):
            fin_copy(index).wait_send()

    for step in range(1, count):
        to = lax.rem(me + step, count)

        @pl.when(upper_used(to, me))
        def _():
            kv_copy(upper_of(me), 1, step, step, to).wait_send()

        @pl.when(lower_used(to, me))
        def _():
            kv_copy(me, 0, step, step, to).wait_send()

    @pl.when(has_next)
    def _():
        for part in (1, 0):
            for g in range(KEY_VALUE_HEADS):
                dq_copy(part, g).wait_recv()
        for index in range(2):
            pltpu.make_async_remote_copy(
                src_ref=fin.at[pl.ds(index, 1)],
                dst_ref=(kg_ref, vg_ref)[index],
                send_sem=fin_send.at[index],
                recv_sem=fin_recv.at[index],
                device_id={"pipe": section + 1},
                device_id_type=MESH,
            ).wait_recv()


def solution(mesh):
    count, sections = mesh.shape["ctx"], mesh.shape["pipe"]

    def local(queries, keys, values, out_grad, doc_blocks):
        rows, columns = queries.shape[1:]
        half = rows // 2
        width = keys.shape[2]
        span = count * half
        heads = columns // HEAD_SIZE
        group = heads // KEY_VALUE_HEADS
        vmem = pl.BlockSpec(memory_space=pltpu.VMEM)
        dma = pltpu.SemaphoreType.DMA
        shape = jax.ShapeDtypeStruct
        return pl.pallas_call(
            functools.partial(kernel, count, sections, heads, doc_blocks.shape[1]),
            out_shape=(
                shape(queries.shape, BF16),
                shape(queries.shape, BF16),
                shape(keys.shape, BF16),
                shape(values.shape, BF16),
            ),
            in_specs=[pl.BlockSpec(memory_space=pltpu.SMEM)] + [vmem] * 4,
            out_specs=(vmem,) * 4,
            scratch_shapes=[
                pltpu.VMEM((2 * span, 2 * width), BF16),
                pltpu.VMEM((2 * span, 2 * width), F32),
                pltpu.VMEM((2 * span, 2 * width), BF16),
                pltpu.VMEM((count, 2, half, 2 * width), BF16),
                pltpu.VMEM((span, group * half), F32),
                pltpu.VMEM(queries.shape, BF16),
                pltpu.VMEM((2, rows, width), BF16),
                dma((count, 2)),
                dma((count, 2)),
                dma((count, 2)),
                dma((count, 2)),
                dma((2 * KEY_VALUE_HEADS,)),
                dma((2 * KEY_VALUE_HEADS,)),
                dma((2,)),
                dma((2,)),
            ],
            compiler_params=pltpu.CompilerParams(
                collective_id=0, has_side_effects=True, vmem_limit_bytes=40 << 20
            ),
        )(doc_blocks, queries, keys, values, out_grad)

    split = P(("dp", "pipe"), "ctx", None)
    return jax.shard_map(
        local,
        mesh=mesh,
        in_specs=(split, split, split, split, P(("dp", "pipe"), None)),
        out_specs=(split,) * 4,
        check_vma=False,
    )
```

```python
import functools
import math

import jax
import jax.numpy as jnp
from jax import lax
from jax.experimental import pallas as pl
from jax.experimental.pallas import tpu as pltpu
from jax.sharding import PartitionSpec as P

KEY_VALUE_HEADS = 2
HEAD_SIZE = 128
BLK = 128
LOG2E = math.log2(math.e)
F32 = jnp.float32
BF16 = jnp.bfloat16


def dot(a, b, contract):
    return lax.dot_general(a, b, (contract, ((), ())), preferred_element_type=F32)


def kernel(
    count, sections, heads, docs,
    doc_in, q_in, k_in, v_in, go_in,
    att_ref, qg_ref, kg_ref, vg_ref,
    doc_ref, q_ref, go_ref, k_ref, v_ref,
    kv, acc, dkv, pair, paired, recv, probs, dq, fin,
    load_sem, line_send, line_recv, side_send, side_recv,
    pair_send, pair_recv, sum_send, sum_recv,
    dq_send, dq_recv, fin_send, fin_recv,
):
    rows = q_ref.shape[1]
    half = rows // 2
    group = heads // KEY_VALUE_HEADS
    lanes = group * half
    span = count * half
    pairs = count // 2
    scale = 1.0 / math.sqrt(HEAD_SIZE)
    me = lax.axis_index("ctx")
    line = me // 2
    side = me % 2
    partner = line * 2 + 1 - side
    section = lax.axis_index("pipe")
    has_grads = section > 0
    has_next = section < sections - 1
    MESH = pl.DeviceIdType.MESH

    loads = [
        pltpu.make_async_copy(source, target, load_sem.at[i])
        for i, (source, target) in enumerate(
            ((k_in, k_ref), (v_in, v_ref), (doc_in, doc_ref), (q_in, q_ref), (go_in, go_ref))
        )
    ]
    for load in loads:
        load.start()

    def block_rows(block):
        return pl.ds(pl.multiple_of(block * half, half), half)

    def start_of(c):
        return 2 * ((2 * count - 1 - c) // 2) - count + 2

    def block_of(d, part):
        return 2 * count - 1 - d if part else d

    def used(c, d, part):
        return c <= d if part else (d <= c) | (d >= start_of(c))

    def used_by_pair(p, d, part):
        return used(2 * p, d, part) | used(2 * p + 1, d, part)

    def ahead(step):
        return lax.rem(line + step, pairs)

    def behind(step):
        return lax.rem(line + pairs - step, pairs)

    kv[...] = jnp.zeros_like(kv)
    pair[...] = jnp.zeros_like(pair)
    recv[...] = jnp.zeros_like(recv)

    @pl.when(jnp.logical_not(has_next))
    def _():
        qg_ref[...] = jnp.zeros_like(qg_ref)
        kg_ref[...] = jnp.zeros_like(kg_ref)
        vg_ref[...] = jnp.zeros_like(vg_ref)

    barrier = pltpu.get_barrier_semaphore()
    for step in range(1, pairs):
        pl.semaphore_signal(
            barrier, inc=1, device_id={"ctx": ahead(step) * 2 + side}, device_id_type=MESH
        )
    pl.semaphore_signal(barrier, inc=1, device_id={"ctx": partner}, device_id_type=MESH)

    @pl.when(has_grads)
    def _():
        pl.semaphore_signal(barrier, inc=1, device_id={"pipe": section - 1}, device_id_type=MESH)

    @pl.when(has_next)
    def _():
        pl.semaphore_signal(barrier, inc=1, device_id={"pipe": section + 1}, device_id_type=MESH)

    loads[0].wait()
    loads[1].wait()
    for part in range(2):
        for g in range(KEY_VALUE_HEADS):
            for ref, at in ((k_ref, 0), (v_ref, 1)):
                kv[g, block_rows(block_of(me, part)), at * HEAD_SIZE:(at + 1) * HEAD_SIZE] = ref[
                    0, part * half:(part + 1) * half, g * HEAD_SIZE:(g + 1) * HEAD_SIZE
                ]

    pl.semaphore_wait(
        barrier, pairs + jnp.minimum(section, 1) + jnp.minimum(sections - 1 - section, 1)
    )

    def remote(source, target, send, receive, axis, device):
        return pltpu.make_async_remote_copy(
            src_ref=source,
            dst_ref=target,
            send_sem=send,
            recv_sem=receive,
            device_id={axis: device},
            device_id_type=MESH,
        )

    def line_copy(g, part, step, owner, target):
        block = kv.at[g, block_rows(block_of(owner, part))]
        at = (g, part, step)
        return remote(block, block, line_send.at[at], line_recv.at[at], "ctx", target)

    def side_copy(g, part, step, owner):
        block = kv.at[g, block_rows(block_of(owner, part))]
        at = (g, part, step)
        return remote(block, block, side_send.at[at], side_recv.at[at], "ctx", partner)

    def send_keys(g, act):
        for part in range(2):
            for step in range(1, pairs):
                @pl.when(used_by_pair(ahead(step), me, part))
                def _():
                    act(line_copy(g, part, step, me, ahead(step) * 2 + side))

            @pl.when(used(partner, me, part))
            def _():
                act(side_copy(g, part, 0, me))

    def pass_keys(g):
        for step in range(1, pairs):
            for part in range(2):
                owner = behind(step) * 2 + side

                @pl.when(used_by_pair(line, owner, part))
                def _():
                    line_copy(g, part, step, owner, owner).wait_recv()

                @pl.when(used(partner, owner, part))
                def _():
                    side_copy(g, part, step, owner).start()

    def wait_passed(g):
        for step in range(pairs):
            for part in range(2):
                owner = behind(step) * 2 + 1 - side

                @pl.when(used(me, owner, part))
                def _():
                    side_copy(g, part, step, owner).wait_recv()

    def wait_pass_sent(g):
        for step in range(1, pairs):
            for part in range(2):
                owner = behind(step) * 2 + side

                @pl.when(used(partner, owner, part))
                def _():
                    side_copy(g, part, step, owner).wait_send()

    for g in range(KEY_VALUE_HEADS):
        send_keys(g, lambda copy: copy.start())
    acc[...] = jnp.zeros_like(acc)
    for load in loads[2:]:
        load.wait()

    def stack(ref, part, g):
        return jnp.concatenate(
            [
                ref[0, part * half:(part + 1) * half, h * HEAD_SIZE:(h + 1) * HEAD_SIZE]
                for h in range(g * group, (g + 1) * group)
            ],
            axis=0,
        )

    def unstack(ref, part, g, value):
        for j in range(group):
            h = g * group + j
            ref[0, part * half:(part + 1) * half, h * HEAD_SIZE:(h + 1) * HEAD_SIZE] = value[
                j * half:(j + 1) * half
            ]

    def dq_copy(part, g):
        index = part * KEY_VALUE_HEADS + g
        cut = (
            slice(None),
            pl.ds(part * half, half),
            pl.ds(g * group * HEAD_SIZE, group * HEAD_SIZE),
        )
        return remote(
            dq.at[cut], qg_ref.at[cut], dq_send.at[index], dq_recv.at[index], "pipe", section - 1
        )

    def fin_copy(g, index):
        target = (kg_ref, vg_ref)[index].at[:, :, pl.ds(g * HEAD_SIZE, HEAD_SIZE)]
        return remote(
            fin.at[g, pl.ds(index, 1)], target,
            fin_send.at[g, index], fin_recv.at[g, index], "pipe", section - 1,
        )

    def unit(part, g):
        first = start_of(me) if part else 0
        own = block_of(me, part)
        base = first * half
        window = pl.ds(pl.multiple_of(base, BLK), span) if part else pl.ds(0, span)
        query = stack(q_ref, part, g)
        grad = stack(go_ref, part, g)
        keys = kv[g, window, :HEAD_SIZE]
        values = kv[g, window, HEAD_SIZE:]
        bound = jnp.int32(0)
        low = jnp.int32(0)
        for j in range(docs - 1):
            bound = bound + doc_ref[0, j] * BLK
            low = jnp.where(bound <= own * half, bound, low)
        key_pos = base + lax.broadcasted_iota(jnp.int32, (span, lanes), 0)
        query_pos = own * half + lax.broadcasted_iota(jnp.int32, (span, lanes), 1) % half
        visible = (key_pos >= low) & (key_pos <= query_pos)
        scores = dot(keys, query, ((1,), (1,))) * (scale * LOG2E)
        scores = jnp.where(visible, scores, -jnp.inf)
        top = jnp.max(scores, axis=0, keepdims=True)
        weights = jnp.exp2(scores - top)
        weights = weights * (1.0 / jnp.sum(weights, axis=0, keepdims=True))
        probs[...] = weights
        low_weights = weights.astype(BF16)
        out = dot(values.T, low_weights, ((1,), (0,))).astype(BF16)
        unstack(att_ref, part, g, out.T)

        @pl.when(has_grads)
        def _():
            delta = jnp.sum(grad.T.astype(F32) * out.astype(F32), axis=0, keepdims=True)
            weight_grad = dot(values, grad, ((1,), (1,)))
            p = probs[...]
            score_grad = (p * (weight_grad - delta) * scale).astype(BF16)
            query_grad = dot(keys.T, score_grad, ((1,), (0,))).astype(BF16)
            unstack(dq, part, g, query_grad.T)
            dq_copy(part, g).start()
            acc[g, window, :HEAD_SIZE] += dot(score_grad, query, ((1,), (0,)))
            acc[g, window, HEAD_SIZE:] += dot(p.astype(BF16), grad, ((1,), (0,)))

    def pair_copy(g, part, step, owner):
        at = (g, part, step)
        return remote(
            dkv.at[g, block_rows(block_of(owner, part))], pair.at[at],
            pair_send.at[at], pair_recv.at[at], "ctx", partner,
        )

    def sum_copy(g, part, step, owner):
        at = (g, part, step)
        return remote(
            paired.at[at], recv.at[at], sum_send.at[at], sum_recv.at[at], "ctx", owner
        )

    def terms_to_partner(g, act):
        for step in (*range(1, pairs), 0):
            for part in range(2):
                owner = ahead(step) * 2 + 1 - side

                @pl.when(used(me, owner, part))
                def _():
                    act(pair_copy(g, part, step, owner))

    def start_terms(g):
        @pl.when(has_grads)
        def _():
            dkv[g] = acc[g].astype(BF16)
            terms_to_partner(g, lambda copy: copy.start())

    def own_and_pair(g, part, step, owner):
        @pl.when(used(partner, owner, part))
        def _():
            pair_copy(g, part, step, owner).wait_recv()

        return dkv[g, block_rows(block_of(owner, part)), :].astype(F32) + pair[
            g, part, step
        ].astype(F32)

    def sums_along_line(g):
        @pl.when(has_grads)
        def _():
            for step in range(1, pairs):
                for part in range(2):
                    owner = ahead(step) * 2 + side

                    @pl.when(used_by_pair(line, owner, part))
                    def _():
                        paired[g, part, step] = own_and_pair(g, part, step, owner).astype(BF16)
                        sum_copy(g, part, step, owner).start()

    def finish(g):
        @pl.when(has_grads)
        def _():
            for part in range(2):
                total = own_and_pair(g, part, 0, me)
                for step in range(1, pairs):
                    @pl.when(used_by_pair(behind(step), me, part))
                    def _():
                        sum_copy(g, part, step, behind(step) * 2 + side).wait_recv()

                    total = total + recv[g, part, step].astype(F32)
                total = total.astype(BF16)
                fin[g, 0, part * half:(part + 1) * half, :] = total[:, :HEAD_SIZE]
                fin[g, 1, part * half:(part + 1) * half, :] = total[:, HEAD_SIZE:]
            for index in range(2):
                fin_copy(g, index).start()

    pass_keys(0)
    wait_passed(0)
    unit(1, 0)
    pass_keys(1)
    unit(0, 0)
    start_terms(0)
    wait_passed(1)
    unit(1, 1)
    sums_along_line(0)
    unit(0, 1)
    start_terms(1)
    finish(0)
    sums_along_line(1)
    finish(1)

    for g in range(KEY_VALUE_HEADS):
        send_keys(g, lambda copy: copy.wait_send())
        wait_pass_sent(g)

    @pl.when(has_grads)
    def _():
        for g in range(KEY_VALUE_HEADS):
            terms_to_partner(g, lambda copy: copy.wait_send())
            for part in range(2):
                for step in range(1, pairs):
                    owner = ahead(step) * 2 + side

                    @pl.when(used_by_pair(line, owner, part))
                    def _():
                        sum_copy(g, part, step, owner).wait_send()

                dq_copy(part, g).wait_send()
                fin_copy(g, part).wait_send()

    @pl.when(has_next)
    def _():
        for g in range(KEY_VALUE_HEADS):
            for part in range(2):
                dq_copy(part, g).wait_recv()
                fin_copy(g, part).wait_recv()


def write_out(*refs):
    size = (len(refs) - 1) // 2
    copies = [
        pltpu.make_async_copy(refs[i], refs[size + i], refs[-1].at[i]) for i in range(size)
    ]
    for copy in copies:
        copy.start()
    for copy in copies:
        copy.wait()


def solution(mesh):
    count, sections = mesh.shape["ctx"], mesh.shape["pipe"]

    def local(queries, keys, values, out_grad, doc_blocks):
        rows, columns = queries.shape[1:]
        half = rows // 2
        span = count * half
        heads = columns // HEAD_SIZE
        group = heads // KEY_VALUE_HEADS
        pairs = count // 2
        vmem = pl.BlockSpec(memory_space=pltpu.VMEM)
        hbm = pl.BlockSpec(memory_space=pltpu.HBM)
        dma = pltpu.SemaphoreType.DMA
        outputs = tuple(
            jax.ShapeDtypeStruct(x.shape, BF16) for x in (queries, queries, keys, values)
        )
        blocks = (KEY_VALUE_HEADS, 2, pairs)
        terms = (KEY_VALUE_HEADS, 2 * span, 2 * HEAD_SIZE)
        results = pl.pallas_call(
            functools.partial(kernel, count, sections, heads, doc_blocks.shape[1]),
            out_shape=outputs,
            in_specs=[hbm] * 5,
            out_specs=(vmem,) * 4,
            scratch_shapes=[
                pltpu.SMEM(doc_blocks.shape, jnp.int32),
                pltpu.VMEM(queries.shape, BF16),
                pltpu.VMEM(queries.shape, BF16),
                pltpu.VMEM(keys.shape, BF16),
                pltpu.VMEM(keys.shape, BF16),
                pltpu.VMEM(terms, BF16),
                pltpu.VMEM(terms, F32),
                pltpu.VMEM(terms, BF16),
                pltpu.VMEM((*blocks, half, 2 * HEAD_SIZE), BF16),
                pltpu.VMEM((*blocks, half, 2 * HEAD_SIZE), BF16),
                pltpu.VMEM((*blocks, half, 2 * HEAD_SIZE), BF16),
                pltpu.VMEM((span, group * half), F32),
                pltpu.VMEM(queries.shape, BF16),
                pltpu.VMEM((KEY_VALUE_HEADS, 2, rows, HEAD_SIZE), BF16),
                dma((5,)),
                *[dma(blocks)] * 8,
                *[dma((2 * KEY_VALUE_HEADS,))] * 2,
                *[dma((KEY_VALUE_HEADS, 2))] * 2,
            ],
            compiler_params=pltpu.CompilerParams(
                collective_id=0, has_side_effects=True, vmem_limit_bytes=40 << 20
            ),
        )(doc_blocks, queries, keys, values, out_grad)
        return pl.pallas_call(
            write_out,
            out_shape=outputs,
            in_specs=[vmem] * 4,
            out_specs=(hbm,) * 4,
            scratch_shapes=[dma((4,))],
        )(*results)

    split = P(("dp", "pipe"), "ctx", None)
    return jax.shard_map(
        local,
        mesh=mesh,
        in_specs=(split, split, split, split, P(("dp", "pipe"), None)),
        out_specs=(split,) * 4,
        check_vma=False,
    )
```

```python
import functools
import math

import jax
import jax.numpy as jnp
from jax import lax
from jax.experimental import pallas as pl
from jax.experimental.pallas import tpu as pltpu
from jax.sharding import PartitionSpec as P

KEY_VALUE_HEADS = 2
HEAD_SIZE = 128
BLK = 128
VMEM_BYTES = 62_000_000
LOG2E = math.log2(math.e)
F32 = jnp.float32
BF16 = jnp.bfloat16


def dot(a, b, contract):
    return lax.dot_general(a, b, (contract, ((), ())), preferred_element_type=F32)


def kernel(
    count, sections, heads, docs,
    doc_in, q_in, k_in, v_in, go_in,
    att_out, qg_ref, kg_ref, vg_ref,
    att_ref, blank, doc_ref, q_ref, go_ref, k_ref, v_ref,
    kv, acc, dkv, pair, paired, recv, probs, dq, fin,
    load_sem, store_sem, line_send, line_recv, side_send, side_recv,
    pair_send, pair_recv, sum_send, sum_recv,
    dq_send, dq_recv, fin_send, fin_recv,
):
    rows = q_ref.shape[1]
    half = rows // 2
    group = heads // KEY_VALUE_HEADS
    lanes = group * half
    span = count * half
    pairs = count // 2
    scale = 1.0 / math.sqrt(HEAD_SIZE)
    me = lax.axis_index("ctx")
    line = me // 2
    side = me % 2
    partner = line * 2 + 1 - side
    section = lax.axis_index("pipe")
    has_grads = section > 0
    has_next = section < sections - 1
    MESH = pl.DeviceIdType.MESH

    loads = [
        pltpu.make_async_copy(source, target, load_sem.at[i])
        for i, (source, target) in enumerate(
            ((k_in, k_ref), (v_in, v_ref), (doc_in, doc_ref), (q_in, q_ref), (go_in, go_ref))
        )
    ]
    for load in loads:
        load.start()

    def block_rows(block):
        return pl.ds(pl.multiple_of(block * half, half), half)

    def start_of(c):
        return 2 * ((2 * count - 1 - c) // 2) - count + 2

    def block_of(d, part):
        return 2 * count - 1 - d if part else d

    def used(c, d, part):
        return c <= d if part else (d <= c) | (d >= start_of(c))

    def used_by_pair(p, d, part):
        return used(2 * p, d, part) | used(2 * p + 1, d, part)

    def ahead(step):
        return lax.rem(line + step, pairs)

    def behind(step):
        return lax.rem(line + pairs - step, pairs)

    kv[...] = jnp.zeros_like(kv)
    pair[...] = jnp.zeros_like(pair)
    recv[...] = jnp.zeros_like(recv)

    barrier = pltpu.get_barrier_semaphore()
    for step in range(1, pairs):
        pl.semaphore_signal(
            barrier, inc=1, device_id={"ctx": ahead(step) * 2 + side}, device_id_type=MESH
        )
    pl.semaphore_signal(barrier, inc=1, device_id={"ctx": partner}, device_id_type=MESH)

    @pl.when(has_grads)
    def _():
        pl.semaphore_signal(barrier, inc=1, device_id={"pipe": section - 1}, device_id_type=MESH)

    @pl.when(has_next)
    def _():
        pl.semaphore_signal(barrier, inc=1, device_id={"pipe": section + 1}, device_id_type=MESH)

    loads[0].wait()
    loads[1].wait()
    for part in range(2):
        for g in range(KEY_VALUE_HEADS):
            for ref, at in ((k_ref, 0), (v_ref, 1)):
                kv[g, block_rows(block_of(me, part)), at * HEAD_SIZE:(at + 1) * HEAD_SIZE] = ref[
                    0, part * half:(part + 1) * half, g * HEAD_SIZE:(g + 1) * HEAD_SIZE
                ]

    pl.semaphore_wait(
        barrier, pairs + jnp.minimum(section, 1) + jnp.minimum(sections - 1 - section, 1)
    )

    def remote(source, target, send, receive, axis, device):
        return pltpu.make_async_remote_copy(
            src_ref=source,
            dst_ref=target,
            send_sem=send,
            recv_sem=receive,
            device_id={axis: device},
            device_id_type=MESH,
        )

    def line_copy(g, part, step, owner, target):
        block = kv.at[g, block_rows(block_of(owner, part))]
        at = (g, part, step)
        return remote(block, block, line_send.at[at], line_recv.at[at], "ctx", target)

    def side_copy(g, part, step, owner):
        block = kv.at[g, block_rows(block_of(owner, part))]
        at = (g, part, step)
        return remote(block, block, side_send.at[at], side_recv.at[at], "ctx", partner)

    def send_keys(g, act):
        for part in range(2):
            for step in range(1, pairs):
                @pl.when(used_by_pair(ahead(step), me, part))
                def _():
                    act(line_copy(g, part, step, me, ahead(step) * 2 + side))

            @pl.when(used(partner, me, part))
            def _():
                act(side_copy(g, part, 0, me))

    def pass_keys(g):
        for step in range(1, pairs):
            for part in range(2):
                owner = behind(step) * 2 + side

                @pl.when(used_by_pair(line, owner, part))
                def _():
                    line_copy(g, part, step, owner, owner).wait_recv()

                @pl.when(used(partner, owner, part))
                def _():
                    side_copy(g, part, step, owner).start()

    def wait_passed(g):
        for step in range(pairs):
            for part in range(2):
                owner = behind(step) * 2 + 1 - side

                @pl.when(used(me, owner, part))
                def _():
                    side_copy(g, part, step, owner).wait_recv()

    def wait_pass_sent(g):
        for step in range(1, pairs):
            for part in range(2):
                owner = behind(step) * 2 + side

                @pl.when(used(partner, owner, part))
                def _():
                    side_copy(g, part, step, owner).wait_send()

    for g in range(KEY_VALUE_HEADS):
        send_keys(g, lambda copy: copy.start())

    columns = k_in.shape[2]
    fills = [
        pltpu.make_async_copy(source, target, store_sem.at[2 * KEY_VALUE_HEADS + i])
        for i, (source, target) in enumerate(
            (
                (blank, qg_ref),
                (blank.at[:, :, pl.ds(0, columns)], kg_ref),
                (blank.at[:, :, pl.ds(0, columns)], vg_ref),
            )
        )
    ]

    @pl.when(jnp.logical_not(has_next))
    def _():
        blank[...] = jnp.zeros_like(blank)
        for fill in fills:
            fill.start()

    acc[...] = jnp.zeros_like(acc)
    for load in loads[2:]:
        load.wait()

    def stack(ref, part, g):
        return jnp.concatenate(
            [
                ref[0, part * half:(part + 1) * half, h * HEAD_SIZE:(h + 1) * HEAD_SIZE]
                for h in range(g * group, (g + 1) * group)
            ],
            axis=0,
        )

    def unstack(ref, part, g, value):
        for j in range(group):
            h = g * group + j
            ref[0, part * half:(part + 1) * half, h * HEAD_SIZE:(h + 1) * HEAD_SIZE] = value[
                j * half:(j + 1) * half
            ]

    def cut_of(part, g):
        return (
            slice(None),
            pl.ds(part * half, half),
            pl.ds(g * group * HEAD_SIZE, group * HEAD_SIZE),
        )

    def att_copy(part, g):
        cut = cut_of(part, g)
        return pltpu.make_async_copy(
            att_ref.at[cut], att_out.at[cut], store_sem.at[part * KEY_VALUE_HEADS + g]
        )

    def dq_copy(part, g):
        index = part * KEY_VALUE_HEADS + g
        cut = cut_of(part, g)
        return remote(
            dq.at[cut], qg_ref.at[cut], dq_send.at[index], dq_recv.at[index], "pipe", section - 1
        )

    def fin_copy(g, index):
        target = (kg_ref, vg_ref)[index].at[:, :, pl.ds(g * HEAD_SIZE, HEAD_SIZE)]
        return remote(
            fin.at[g, pl.ds(index, 1)], target,
            fin_send.at[g, index], fin_recv.at[g, index], "pipe", section - 1,
        )

    def unit(part, g):
        first = start_of(me) if part else 0
        own = block_of(me, part)
        base = first * half
        window = pl.ds(pl.multiple_of(base, BLK), span) if part else pl.ds(0, span)
        query = stack(q_ref, part, g)
        grad = stack(go_ref, part, g)
        keys = kv[g, window, :HEAD_SIZE]
        values = kv[g, window, HEAD_SIZE:]
        bound = jnp.int32(0)
        low = jnp.int32(0)
        for j in range(docs - 1):
            bound = bound + doc_ref[0, j] * BLK
            low = jnp.where(bound <= own * half, bound, low)
        key_pos = base + lax.broadcasted_iota(jnp.int32, (span, lanes), 0)
        query_pos = own * half + lax.broadcasted_iota(jnp.int32, (span, lanes), 1) % half
        visible = (key_pos >= low) & (key_pos <= query_pos)
        scores = dot(keys, query, ((1,), (1,))) * (scale * LOG2E)
        scores = jnp.where(visible, scores, -jnp.inf)
        top = jnp.max(scores, axis=0, keepdims=True)
        weights = jnp.exp2(scores - top)
        weights = weights * (1.0 / jnp.sum(weights, axis=0, keepdims=True))
        probs[...] = weights
        low_weights = weights.astype(BF16)
        out = dot(values.T, low_weights, ((1,), (0,))).astype(BF16)
        unstack(att_ref, part, g, out.T)
        att_copy(part, g).start()

        @pl.when(has_grads)
        def _():
            delta = jnp.sum(grad.T.astype(F32) * out.astype(F32), axis=0, keepdims=True)
            weight_grad = dot(values, grad, ((1,), (1,)))
            p = probs[...]
            score_grad = (p * (weight_grad - delta) * scale).astype(BF16)
            query_grad = dot(keys.T, score_grad, ((1,), (0,))).astype(BF16)
            unstack(dq, part, g, query_grad.T)
            dq_copy(part, g).start()
            acc[g, window, :HEAD_SIZE] += dot(score_grad, query, ((1,), (0,)))
            acc[g, window, HEAD_SIZE:] += dot(p.astype(BF16), grad, ((1,), (0,)))

    def pair_copy(g, part, step, owner):
        at = (g, part, step)
        return remote(
            dkv.at[g, block_rows(block_of(owner, part))], pair.at[at],
            pair_send.at[at], pair_recv.at[at], "ctx", partner,
        )

    def sum_copy(g, part, step, owner):
        at = (g, part, step)
        return remote(
            paired.at[at], recv.at[at], sum_send.at[at], sum_recv.at[at], "ctx", owner
        )

    def terms_to_partner(g, act):
        for step in (*range(1, pairs), 0):
            for part in range(2):
                owner = ahead(step) * 2 + 1 - side

                @pl.when(used(me, owner, part))
                def _():
                    act(pair_copy(g, part, step, owner))

    def start_terms(g):
        @pl.when(has_grads)
        def _():
            dkv[g] = acc[g].astype(BF16)
            terms_to_partner(g, lambda copy: copy.start())

    def own_and_pair(g, part, step, owner):
        @pl.when(used(partner, owner, part))
        def _():
            pair_copy(g, part, step, owner).wait_recv()

        return dkv[g, block_rows(block_of(owner, part)), :].astype(F32) + pair[
            g, part, step
        ].astype(F32)

    def sums_along_line(g):
        @pl.when(has_grads)
        def _():
            for step in range(1, pairs):
                for part in range(2):
                    owner = ahead(step) * 2 + side

                    @pl.when(used_by_pair(line, owner, part))
                    def _():
                        paired[g, part, step] = own_and_pair(g, part, step, owner).astype(BF16)
                        sum_copy(g, part, step, owner).start()

    def finish(g):
        @pl.when(has_grads)
        def _():
            for part in range(2):
                total = own_and_pair(g, part, 0, me)
                for step in range(1, pairs):
                    @pl.when(used_by_pair(behind(step), me, part))
                    def _():
                        sum_copy(g, part, step, behind(step) * 2 + side).wait_recv()

                    total = total + recv[g, part, step].astype(F32)
                total = total.astype(BF16)
                fin[g, 0, part * half:(part + 1) * half, :] = total[:, :HEAD_SIZE]
                fin[g, 1, part * half:(part + 1) * half, :] = total[:, HEAD_SIZE:]
            for index in range(2):
                fin_copy(g, index).start()

    pass_keys(0)
    wait_passed(0)
    unit(1, 0)
    pass_keys(1)
    unit(0, 0)
    start_terms(0)
    wait_passed(1)
    unit(1, 1)
    sums_along_line(0)
    unit(0, 1)
    start_terms(1)
    finish(0)
    sums_along_line(1)
    finish(1)

    for part in range(2):
        for g in range(KEY_VALUE_HEADS):
            att_copy(part, g).wait()

    @pl.when(jnp.logical_not(has_next))
    def _():
        for fill in fills:
            fill.wait()

    for g in range(KEY_VALUE_HEADS):
        send_keys(g, lambda copy: copy.wait_send())
        wait_pass_sent(g)

    @pl.when(has_grads)
    def _():
        for g in range(KEY_VALUE_HEADS):
            terms_to_partner(g, lambda copy: copy.wait_send())
            for part in range(2):
                for step in range(1, pairs):
                    owner = ahead(step) * 2 + side

                    @pl.when(used_by_pair(line, owner, part))
                    def _():
                        sum_copy(g, part, step, owner).wait_send()

                dq_copy(part, g).wait_send()
                fin_copy(g, part).wait_send()

    @pl.when(has_next)
    def _():
        for g in range(KEY_VALUE_HEADS):
            for part in range(2):
                dq_copy(part, g).wait_recv()
                fin_copy(g, part).wait_recv()


def write_out(*refs):
    size = (len(refs) - 1) // 2
    copies = [
        pltpu.make_async_copy(refs[i], refs[size + i], refs[-1].at[i]) for i in range(size)
    ]
    for copy in copies:
        copy.start()
    for copy in copies:
        copy.wait()


def solution(mesh):
    count, sections = mesh.shape["ctx"], mesh.shape["pipe"]

    def local(queries, keys, values, out_grad, doc_blocks):
        rows, columns = queries.shape[1:]
        half = rows // 2
        span = count * half
        heads = columns // HEAD_SIZE
        group = heads // KEY_VALUE_HEADS
        pairs = count // 2
        hbm = pl.BlockSpec(memory_space=pltpu.HBM)
        dma = pltpu.SemaphoreType.DMA
        outputs = tuple(
            jax.ShapeDtypeStruct(x.shape, BF16) for x in (queries, queries, keys, values)
        )
        blocks = (KEY_VALUE_HEADS, 2, pairs)
        terms = (KEY_VALUE_HEADS, 2 * span, 2 * HEAD_SIZE)
        results = pl.pallas_call(
            functools.partial(kernel, count, sections, heads, doc_blocks.shape[1]),
            out_shape=outputs,
            in_specs=[hbm] * 5,
            out_specs=(hbm,) * 4,
            scratch_shapes=[
                pltpu.VMEM(queries.shape, BF16),
                pltpu.VMEM(queries.shape, BF16),
                pltpu.SMEM(doc_blocks.shape, jnp.int32),
                pltpu.VMEM(queries.shape, BF16),
                pltpu.VMEM(queries.shape, BF16),
                pltpu.VMEM(keys.shape, BF16),
                pltpu.VMEM(keys.shape, BF16),
                pltpu.VMEM(terms, BF16),
                pltpu.VMEM(terms, F32),
                pltpu.VMEM(terms, BF16),
                pltpu.VMEM((*blocks, half, 2 * HEAD_SIZE), BF16),
                pltpu.VMEM((*blocks, half, 2 * HEAD_SIZE), BF16),
                pltpu.VMEM((*blocks, half, 2 * HEAD_SIZE), BF16),
                pltpu.VMEM((span, group * half), F32),
                pltpu.VMEM(queries.shape, BF16),
                pltpu.VMEM((KEY_VALUE_HEADS, 2, rows, HEAD_SIZE), BF16),
                dma((5,)),
                dma((2 * KEY_VALUE_HEADS + 3,)),
                *[dma(blocks)] * 8,
                *[dma((2 * KEY_VALUE_HEADS,))] * 2,
                *[dma((KEY_VALUE_HEADS, 2))] * 2,
            ],
            compiler_params=pltpu.CompilerParams(
                collective_id=0, has_side_effects=True, vmem_limit_bytes=VMEM_BYTES
            ),
        )(doc_blocks, queries, keys, values, out_grad)
        return pl.pallas_call(
            write_out,
            out_shape=outputs,
            in_specs=[hbm] * 4,
            out_specs=(hbm,) * 4,
            scratch_shapes=[dma((4,))],
            compiler_params=pltpu.CompilerParams(vmem_limit_bytes=VMEM_BYTES),
        )(*results)

    split = P(("dp", "pipe"), "ctx", None)
    return jax.shard_map(
        local,
        mesh=mesh,
        in_specs=(split, split, split, split, P(("dp", "pipe"), None)),
        out_specs=(split,) * 4,
        check_vma=False,
    )
```

```python
import functools
import math

import jax
import jax.numpy as jnp
from jax import lax
from jax.experimental import pallas as pl
from jax.experimental.pallas import tpu as pltpu
from jax.sharding import PartitionSpec as P

KEY_VALUE_HEADS = 2
HEAD_SIZE = 128
BLK = 128
VMEM_BYTES = 62_000_000
LOG2E = math.log2(math.e)
F32 = jnp.float32
BF16 = jnp.bfloat16


def dot(a, b, contract):
    return lax.dot_general(a, b, (contract, ((), ())), preferred_element_type=F32)


def kernel(
    count, sections, heads, docs,
    doc_in, q_in, k_in, v_in, go_in,
    att_out, qg_ref, kg_ref, vg_ref,
    att_ref, blank, doc_ref, q_ref, go_ref, k_ref, v_ref,
    kv, acc, dkv, pair, paired, recv, probs, dq, fin,
    load_sem, store_sem, line_send, line_recv, side_send, side_recv,
    pair_send, pair_recv, sum_send, sum_recv,
    dq_send, dq_recv, fin_send, fin_recv,
):
    rows = q_ref.shape[1]
    half = rows // 2
    group = heads // KEY_VALUE_HEADS
    lanes = group * half
    span = count * half
    pairs = count // 2
    scale = 1.0 / math.sqrt(HEAD_SIZE)
    me = lax.axis_index("ctx")
    line = me // 2
    side = me % 2
    partner = line * 2 + 1 - side
    section = lax.axis_index("pipe")
    has_grads = section > 0
    has_next = section < sections - 1
    MESH = pl.DeviceIdType.MESH

    loads = [
        pltpu.make_async_copy(source, target, load_sem.at[i])
        for i, (source, target) in enumerate(
            ((k_in, k_ref), (v_in, v_ref), (doc_in, doc_ref), (q_in, q_ref), (go_in, go_ref))
        )
    ]
    for load in loads:
        load.start()

    def block_rows(block):
        return pl.ds(pl.multiple_of(block * half, half), half)

    def start_of(c):
        return 2 * ((2 * count - 1 - c) // 2) - count + 2

    def block_of(d, part):
        return 2 * count - 1 - d if part else d

    def used(c, d, part):
        return c <= d if part else (d <= c) | (d >= start_of(c))

    def used_by_pair(p, d, part):
        return used(2 * p, d, part) | used(2 * p + 1, d, part)

    def ahead(step):
        return lax.rem(line + step, pairs)

    def behind(step):
        return lax.rem(line + pairs - step, pairs)

    kv[...] = jnp.zeros_like(kv)
    pair[...] = jnp.zeros_like(pair)
    recv[...] = jnp.zeros_like(recv)

    barrier = pltpu.get_barrier_semaphore()
    for step in range(1, pairs):
        pl.semaphore_signal(
            barrier, inc=1, device_id={"ctx": ahead(step) * 2 + side}, device_id_type=MESH
        )
    pl.semaphore_signal(barrier, inc=1, device_id={"ctx": partner}, device_id_type=MESH)

    @pl.when(has_grads)
    def _():
        pl.semaphore_signal(barrier, inc=1, device_id={"pipe": section - 1}, device_id_type=MESH)

    @pl.when(has_next)
    def _():
        pl.semaphore_signal(barrier, inc=1, device_id={"pipe": section + 1}, device_id_type=MESH)

    loads[0].wait()
    loads[1].wait()
    for part in range(2):
        for g in range(KEY_VALUE_HEADS):
            for ref, at in ((k_ref, 0), (v_ref, 1)):
                kv[g, block_rows(block_of(me, part)), at * HEAD_SIZE:(at + 1) * HEAD_SIZE] = ref[
                    0, part * half:(part + 1) * half, g * HEAD_SIZE:(g + 1) * HEAD_SIZE
                ]

    pl.semaphore_wait(
        barrier, pairs + jnp.minimum(section, 1) + jnp.minimum(sections - 1 - section, 1)
    )

    def remote(source, target, send, receive, axis, device):
        return pltpu.make_async_remote_copy(
            src_ref=source,
            dst_ref=target,
            send_sem=send,
            recv_sem=receive,
            device_id={axis: device},
            device_id_type=MESH,
        )

    def line_copy(g, part, step, owner, target):
        block = kv.at[g, block_rows(block_of(owner, part))]
        at = (g, part, step)
        return remote(block, block, line_send.at[at], line_recv.at[at], "ctx", target)

    def side_copy(g, part, step, owner):
        block = kv.at[g, block_rows(block_of(owner, part))]
        at = (g, part, step)
        return remote(block, block, side_send.at[at], side_recv.at[at], "ctx", partner)

    def send_keys(g, act):
        for part in range(2):
            for step in range(1, pairs):
                @pl.when(used_by_pair(ahead(step), me, part))
                def _():
                    act(line_copy(g, part, step, me, ahead(step) * 2 + side))

            @pl.when(used(partner, me, part))
            def _():
                act(side_copy(g, part, 0, me))

    def pass_keys(g):
        for step in range(1, pairs):
            for part in range(2):
                owner = behind(step) * 2 + side

                @pl.when(used_by_pair(line, owner, part))
                def _():
                    line_copy(g, part, step, owner, owner).wait_recv()

                @pl.when(used(partner, owner, part))
                def _():
                    side_copy(g, part, step, owner).start()

    def wait_passed(g):
        for step in range(pairs):
            for part in range(2):
                owner = behind(step) * 2 + 1 - side

                @pl.when(used(me, owner, part))
                def _():
                    side_copy(g, part, step, owner).wait_recv()

    def wait_pass_sent(g):
        for step in range(1, pairs):
            for part in range(2):
                owner = behind(step) * 2 + side

                @pl.when(used(partner, owner, part))
                def _():
                    side_copy(g, part, step, owner).wait_send()

    for g in range(KEY_VALUE_HEADS):
        send_keys(g, lambda copy: copy.start())

    columns = k_in.shape[2]
    fills = [
        pltpu.make_async_copy(source, target, store_sem.at[2 * KEY_VALUE_HEADS + i])
        for i, (source, target) in enumerate(
            (
                (blank, qg_ref),
                (blank.at[:, :, pl.ds(0, columns)], kg_ref),
                (blank.at[:, :, pl.ds(0, columns)], vg_ref),
            )
        )
    ]

    @pl.when(jnp.logical_not(has_next))
    def _():
        blank[...] = jnp.zeros_like(blank)
        for fill in fills:
            fill.start()

    acc[...] = jnp.zeros_like(acc)
    for load in loads[2:]:
        load.wait()

    def stack(ref, part, g):
        return jnp.concatenate(
            [
                ref[0, part * half:(part + 1) * half, h * HEAD_SIZE:(h + 1) * HEAD_SIZE]
                for h in range(g * group, (g + 1) * group)
            ],
            axis=0,
        )

    def unstack(ref, part, g, value):
        for j in range(group):
            h = g * group + j
            ref[0, part * half:(part + 1) * half, h * HEAD_SIZE:(h + 1) * HEAD_SIZE] = value[
                j * half:(j + 1) * half
            ]

    def cut_of(part, g):
        return (
            slice(None),
            pl.ds(part * half, half),
            pl.ds(g * group * HEAD_SIZE, group * HEAD_SIZE),
        )

    def att_copy(part, g):
        cut = cut_of(part, g)
        return pltpu.make_async_copy(
            att_ref.at[cut], att_out.at[cut], store_sem.at[part * KEY_VALUE_HEADS + g]
        )

    def dq_copy(part, g):
        index = part * KEY_VALUE_HEADS + g
        cut = cut_of(part, g)
        return remote(
            dq.at[cut], qg_ref.at[cut], dq_send.at[index], dq_recv.at[index], "pipe", section - 1
        )

    def fin_copy(g, index):
        target = (kg_ref, vg_ref)[index].at[:, :, pl.ds(g * HEAD_SIZE, HEAD_SIZE)]
        return remote(
            fin.at[g, pl.ds(index, 1)], target,
            fin_send.at[g, index], fin_recv.at[g, index], "pipe", section - 1,
        )

    def unit(part, g):
        first = start_of(me) if part else 0
        own = block_of(me, part)
        base = first * half
        window = pl.ds(pl.multiple_of(base, BLK), span) if part else pl.ds(0, span)
        query = stack(q_ref, part, g)
        grad = stack(go_ref, part, g)
        keys = kv[g, window, :HEAD_SIZE]
        values = kv[g, window, HEAD_SIZE:]
        bound = jnp.int32(0)
        low = jnp.int32(0)
        for j in range(docs - 1):
            bound = bound + doc_ref[0, j] * BLK
            low = jnp.where(bound <= own * half, bound, low)
        key_pos = base + lax.broadcasted_iota(jnp.int32, (span, lanes), 0)
        query_pos = own * half + lax.broadcasted_iota(jnp.int32, (span, lanes), 1) % half
        visible = (key_pos >= low) & (key_pos <= query_pos)
        scores = dot(keys, query, ((1,), (1,))) * (scale * LOG2E)
        scores = jnp.where(visible, scores, -jnp.inf)
        top = jnp.max(scores, axis=0, keepdims=True)
        weights = jnp.exp2(scores - top)
        weights = weights * (1.0 / jnp.sum(weights, axis=0, keepdims=True))
        probs[...] = weights
        low_weights = weights.astype(BF16)
        out = dot(values.T, low_weights, ((1,), (0,))).astype(BF16)
        unstack(att_ref, part, g, out.T)
        att_copy(part, g).start()

        @pl.when(has_grads)
        def _():
            delta = jnp.sum(grad.T.astype(F32) * out.astype(F32), axis=0, keepdims=True)
            weight_grad = dot(values, grad, ((1,), (1,)))
            p = probs[...]
            score_grad = (p * (weight_grad - delta) * scale).astype(BF16)
            query_grad = dot(keys.T, score_grad, ((1,), (0,))).astype(BF16)
            unstack(dq, part, g, query_grad.T)
            dq_copy(part, g).start()
            acc[g, window, :HEAD_SIZE] += dot(score_grad, query, ((1,), (0,)))
            acc[g, window, HEAD_SIZE:] += dot(p.astype(BF16), grad, ((1,), (0,)))

    def pair_copy(g, part, step, owner):
        at = (g, part, step)
        return remote(
            dkv.at[g, block_rows(block_of(owner, part))], pair.at[at],
            pair_send.at[at], pair_recv.at[at], "ctx", partner,
        )

    def sum_copy(g, part, step, owner):
        at = (g, part, step)
        return remote(
            paired.at[at], recv.at[at], sum_send.at[at], sum_recv.at[at], "ctx", owner
        )

    def terms_to_partner(g, act):
        for step in (*range(1, pairs), 0):
            for part in range(2):
                owner = ahead(step) * 2 + 1 - side

                @pl.when(used(me, owner, part))
                def _():
                    act(pair_copy(g, part, step, owner))

    def start_terms(g):
        @pl.when(has_grads)
        def _():
            dkv[g] = acc[g].astype(BF16)
            terms_to_partner(g, lambda copy: copy.start())

    def own_and_pair(g, part, step, owner):
        @pl.when(used(partner, owner, part))
        def _():
            pair_copy(g, part, step, owner).wait_recv()

        return dkv[g, block_rows(block_of(owner, part)), :].astype(F32) + pair[
            g, part, step
        ].astype(F32)

    def sums_along_line(g):
        @pl.when(has_grads)
        def _():
            for step in range(1, pairs):
                for part in range(2):
                    owner = ahead(step) * 2 + side

                    @pl.when(used_by_pair(line, owner, part))
                    def _():
                        paired[g, part, step] = own_and_pair(g, part, step, owner).astype(BF16)
                        sum_copy(g, part, step, owner).start()

    def finish(g):
        @pl.when(has_grads)
        def _():
            for part in range(2):
                total = own_and_pair(g, part, 0, me)
                for step in range(1, pairs):
                    @pl.when(used_by_pair(behind(step), me, part))
                    def _():
                        sum_copy(g, part, step, behind(step) * 2 + side).wait_recv()

                    total = total + recv[g, part, step].astype(F32)
                total = total.astype(BF16)
                fin[g, 0, part * half:(part + 1) * half, :] = total[:, :HEAD_SIZE]
                fin[g, 1, part * half:(part + 1) * half, :] = total[:, HEAD_SIZE:]
            for index in range(2):
                fin_copy(g, index).start()

    pass_keys(0)
    wait_passed(0)
    unit(1, 0)
    pass_keys(1)
    unit(0, 0)
    start_terms(0)
    wait_passed(1)
    unit(1, 1)
    sums_along_line(0)
    unit(0, 1)
    start_terms(1)
    finish(0)
    sums_along_line(1)
    finish(1)

    for part in range(2):
        for g in range(KEY_VALUE_HEADS):
            att_copy(part, g).wait()

    @pl.when(jnp.logical_not(has_next))
    def _():
        for fill in fills:
            fill.wait()

    for g in range(KEY_VALUE_HEADS):
        send_keys(g, lambda copy: copy.wait_send())
        wait_pass_sent(g)

    @pl.when(has_grads)
    def _():
        for g in range(KEY_VALUE_HEADS):
            terms_to_partner(g, lambda copy: copy.wait_send())
            for part in range(2):
                for step in range(1, pairs):
                    owner = ahead(step) * 2 + side

                    @pl.when(used_by_pair(line, owner, part))
                    def _():
                        sum_copy(g, part, step, owner).wait_send()

                dq_copy(part, g).wait_send()
                fin_copy(g, part).wait_send()

    @pl.when(has_next)
    def _():
        for g in range(KEY_VALUE_HEADS):
            for part in range(2):
                dq_copy(part, g).wait_recv()
                fin_copy(g, part).wait_recv()


def write_out(*refs):
    size = (len(refs) - 2) // 3
    sources, targets, held = (refs[k * size:(k + 1) * size] for k in range(3))
    load_sem, store_sem = refs[-2:]
    loads = [
        pltpu.make_async_copy(sources[i], held[i], load_sem.at[i]) for i in range(size)
    ]
    stores = [
        pltpu.make_async_copy(held[i], targets[i], store_sem.at[i]) for i in range(size)
    ]
    for load in loads:
        load.start()
    for load, store in zip(loads, stores):
        load.wait()
        store.start()
    for store in stores:
        store.wait()


def solution(mesh):
    count, sections = mesh.shape["ctx"], mesh.shape["pipe"]

    def local(queries, keys, values, out_grad, doc_blocks):
        rows, columns = queries.shape[1:]
        half = rows // 2
        span = count * half
        heads = columns // HEAD_SIZE
        group = heads // KEY_VALUE_HEADS
        pairs = count // 2
        hbm = pl.BlockSpec(memory_space=pltpu.HBM)
        dma = pltpu.SemaphoreType.DMA
        outputs = tuple(
            jax.ShapeDtypeStruct(x.shape, BF16) for x in (queries, queries, keys, values)
        )
        blocks = (KEY_VALUE_HEADS, 2, pairs)
        terms = (KEY_VALUE_HEADS, 2 * span, 2 * HEAD_SIZE)
        results = pl.pallas_call(
            functools.partial(kernel, count, sections, heads, doc_blocks.shape[1]),
            out_shape=outputs,
            in_specs=[hbm] * 5,
            out_specs=(hbm,) * 4,
            scratch_shapes=[
                pltpu.VMEM(queries.shape, BF16),
                pltpu.VMEM(queries.shape, BF16),
                pltpu.SMEM(doc_blocks.shape, jnp.int32),
                pltpu.VMEM(queries.shape, BF16),
                pltpu.VMEM(queries.shape, BF16),
                pltpu.VMEM(keys.shape, BF16),
                pltpu.VMEM(keys.shape, BF16),
                pltpu.VMEM(terms, BF16),
                pltpu.VMEM(terms, F32),
                pltpu.VMEM(terms, BF16),
                pltpu.VMEM((*blocks, half, 2 * HEAD_SIZE), BF16),
                pltpu.VMEM((*blocks, half, 2 * HEAD_SIZE), BF16),
                pltpu.VMEM((*blocks, half, 2 * HEAD_SIZE), BF16),
                pltpu.VMEM((span, group * half), F32),
                pltpu.VMEM(queries.shape, BF16),
                pltpu.VMEM((KEY_VALUE_HEADS, 2, rows, HEAD_SIZE), BF16),
                dma((5,)),
                dma((2 * KEY_VALUE_HEADS + 3,)),
                *[dma(blocks)] * 8,
                *[dma((2 * KEY_VALUE_HEADS,))] * 2,
                *[dma((KEY_VALUE_HEADS, 2))] * 2,
            ],
            compiler_params=pltpu.CompilerParams(
                collective_id=0, has_side_effects=True, vmem_limit_bytes=VMEM_BYTES
            ),
        )(doc_blocks, queries, keys, values, out_grad)
        return pl.pallas_call(
            write_out,
            out_shape=outputs,
            in_specs=[hbm] * 4,
            out_specs=(hbm,) * 4,
            scratch_shapes=[pltpu.VMEM(x.shape, BF16) for x in outputs] + [dma((4,))] * 2,
            compiler_params=pltpu.CompilerParams(vmem_limit_bytes=VMEM_BYTES),
        )(*results)

    split = P(("dp", "pipe"), "ctx", None)
    return jax.shard_map(
        local,
        mesh=mesh,
        in_specs=(split, split, split, split, P(("dp", "pipe"), None)),
        out_specs=(split,) * 4,
        check_vma=False,
    )
```

```python
import functools
import math

import jax
import jax.numpy as jnp
from jax import lax
from jax.experimental import pallas as pl
from jax.experimental.pallas import tpu as pltpu
from jax.sharding import PartitionSpec as P

KEY_VALUE_HEADS = 2
HEAD_SIZE = 128
BLK = 128
VMEM_BYTES = 62_000_000
LOG2E = math.log2(math.e)
F32 = jnp.float32
BF16 = jnp.bfloat16


def dot(a, b, contract):
    return lax.dot_general(a, b, (contract, ((), ())), preferred_element_type=F32)


def kernel(
    count, sections, heads, docs,
    doc_in, q_in, k_in, v_in, go_in,
    att_out, qg_ref, kg_ref, vg_ref,
    att_ref, blank, doc_ref, q_ref, go_ref, k_ref, v_ref,
    kv, acc, dkv, pair, paired, recv, probs, dq, fin,
    load_sem, store_sem, line_send, line_recv, side_send, side_recv,
    pair_send, pair_recv, sum_send, sum_recv,
    dq_send, dq_recv, fin_send, fin_recv,
):
    rows = q_ref.shape[1]
    half = rows // 2
    group = heads // KEY_VALUE_HEADS
    lanes = group * half
    span = count * half
    pairs = count // 2
    scale = 1.0 / math.sqrt(HEAD_SIZE)
    me = lax.axis_index("ctx")
    line = me // 2
    side = me % 2
    partner = line * 2 + 1 - side
    section = lax.axis_index("pipe")
    has_grads = section > 0
    has_next = section < sections - 1
    MESH = pl.DeviceIdType.MESH

    loads = [
        pltpu.make_async_copy(source, target, load_sem.at[i])
        for i, (source, target) in enumerate(
            ((k_in, k_ref), (v_in, v_ref), (doc_in, doc_ref), (q_in, q_ref), (go_in, go_ref))
        )
    ]
    for load in loads:
        load.start()

    def block_rows(block):
        return pl.ds(pl.multiple_of(block * half, half), half)

    def start_of(c):
        return 2 * ((2 * count - 1 - c) // 2) - count + 2

    def block_of(d, part):
        return 2 * count - 1 - d if part else d

    def used(c, d, part):
        return c <= d if part else (d <= c) | (d >= start_of(c))

    def used_by_pair(p, d, part):
        return used(2 * p, d, part) | used(2 * p + 1, d, part)

    def ahead(step):
        return lax.rem(line + step, pairs)

    def behind(step):
        return lax.rem(line + pairs - step, pairs)

    kv[...] = jnp.zeros_like(kv)
    pair[...] = jnp.zeros_like(pair)
    recv[...] = jnp.zeros_like(recv)

    barrier = pltpu.get_barrier_semaphore()
    for step in range(1, pairs):
        pl.semaphore_signal(
            barrier, inc=1, device_id={"ctx": ahead(step) * 2 + side}, device_id_type=MESH
        )
    pl.semaphore_signal(barrier, inc=1, device_id={"ctx": partner}, device_id_type=MESH)

    @pl.when(has_grads)
    def _():
        pl.semaphore_signal(barrier, inc=1, device_id={"pipe": section - 1}, device_id_type=MESH)

    @pl.when(has_next)
    def _():
        pl.semaphore_signal(barrier, inc=1, device_id={"pipe": section + 1}, device_id_type=MESH)

    loads[0].wait()
    loads[1].wait()
    for part in range(2):
        for g in range(KEY_VALUE_HEADS):
            for ref, at in ((k_ref, 0), (v_ref, 1)):
                kv[g, block_rows(block_of(me, part)), at * HEAD_SIZE:(at + 1) * HEAD_SIZE] = ref[
                    0, part * half:(part + 1) * half, g * HEAD_SIZE:(g + 1) * HEAD_SIZE
                ]

    pl.semaphore_wait(
        barrier, pairs + jnp.minimum(section, 1) + jnp.minimum(sections - 1 - section, 1)
    )

    def remote(source, target, send, receive, axis, device):
        return pltpu.make_async_remote_copy(
            src_ref=source,
            dst_ref=target,
            send_sem=send,
            recv_sem=receive,
            device_id={axis: device},
            device_id_type=MESH,
        )

    def line_copy(g, part, step, owner, target):
        block = kv.at[g, block_rows(block_of(owner, part))]
        at = (g, part, step)
        return remote(block, block, line_send.at[at], line_recv.at[at], "ctx", target)

    def side_copy(g, part, step, owner):
        block = kv.at[g, block_rows(block_of(owner, part))]
        at = (g, part, step)
        return remote(block, block, side_send.at[at], side_recv.at[at], "ctx", partner)

    def send_keys(g, act):
        for part in range(2):
            for step in range(1, pairs):
                @pl.when(used_by_pair(ahead(step), me, part))
                def _():
                    act(line_copy(g, part, step, me, ahead(step) * 2 + side))

            @pl.when(used(partner, me, part))
            def _():
                act(side_copy(g, part, 0, me))

    def pass_keys(g):
        for step in range(1, pairs):
            for part in range(2):
                owner = behind(step) * 2 + side

                @pl.when(used_by_pair(line, owner, part))
                def _():
                    line_copy(g, part, step, owner, owner).wait_recv()

                @pl.when(used(partner, owner, part))
                def _():
                    side_copy(g, part, step, owner).start()

    def wait_passed(g):
        for step in range(pairs):
            for part in range(2):
                owner = behind(step) * 2 + 1 - side

                @pl.when(used(me, owner, part))
                def _():
                    side_copy(g, part, step, owner).wait_recv()

    def wait_pass_sent(g):
        for step in range(1, pairs):
            for part in range(2):
                owner = behind(step) * 2 + side

                @pl.when(used(partner, owner, part))
                def _():
                    side_copy(g, part, step, owner).wait_send()

    send_keys(0, lambda copy: copy.start())

    columns = k_in.shape[2]
    fills = [
        pltpu.make_async_copy(source, target, store_sem.at[2 * KEY_VALUE_HEADS + i])
        for i, (source, target) in enumerate(
            (
                (blank, qg_ref),
                (blank.at[:, :, pl.ds(0, columns)], kg_ref),
                (blank.at[:, :, pl.ds(0, columns)], vg_ref),
            )
        )
    ]

    @pl.when(jnp.logical_not(has_next))
    def _():
        blank[...] = jnp.zeros_like(blank)
        for fill in fills:
            fill.start()

    acc[...] = jnp.zeros_like(acc)
    for load in loads[2:]:
        load.wait()

    def stack(ref, part, g):
        return jnp.concatenate(
            [
                ref[0, part * half:(part + 1) * half, h * HEAD_SIZE:(h + 1) * HEAD_SIZE]
                for h in range(g * group, (g + 1) * group)
            ],
            axis=0,
        )

    def unstack(ref, part, g, value):
        for j in range(group):
            h = g * group + j
            ref[0, part * half:(part + 1) * half, h * HEAD_SIZE:(h + 1) * HEAD_SIZE] = value[
                j * half:(j + 1) * half
            ]

    def cut_of(part, g):
        return (
            slice(None),
            pl.ds(part * half, half),
            pl.ds(g * group * HEAD_SIZE, group * HEAD_SIZE),
        )

    def att_copy(part, g):
        cut = cut_of(part, g)
        return pltpu.make_async_copy(
            att_ref.at[cut], att_out.at[cut], store_sem.at[part * KEY_VALUE_HEADS + g]
        )

    def dq_copy(part, g):
        index = part * KEY_VALUE_HEADS + g
        cut = cut_of(part, g)
        return remote(
            dq.at[cut], qg_ref.at[cut], dq_send.at[index], dq_recv.at[index], "pipe", section - 1
        )

    def fin_copy(g, index):
        target = (kg_ref, vg_ref)[index].at[:, :, pl.ds(g * HEAD_SIZE, HEAD_SIZE)]
        return remote(
            fin.at[g, pl.ds(index, 1)], target,
            fin_send.at[g, index], fin_recv.at[g, index], "pipe", section - 1,
        )

    def unit(part, g):
        first = start_of(me) if part else 0
        own = block_of(me, part)
        base = first * half
        window = pl.ds(pl.multiple_of(base, BLK), span) if part else pl.ds(0, span)
        query = stack(q_ref, part, g)
        grad = stack(go_ref, part, g)
        keys = kv[g, window, :HEAD_SIZE]
        values = kv[g, window, HEAD_SIZE:]
        bound = jnp.int32(0)
        low = jnp.int32(0)
        for j in range(docs - 1):
            bound = bound + doc_ref[0, j] * BLK
            low = jnp.where(bound <= own * half, bound, low)
        key_pos = base + lax.broadcasted_iota(jnp.int32, (span, lanes), 0)
        query_pos = own * half + lax.broadcasted_iota(jnp.int32, (span, lanes), 1) % half
        visible = (key_pos >= low) & (key_pos <= query_pos)
        scores = dot(keys, query, ((1,), (1,))) * (scale * LOG2E)
        scores = jnp.where(visible, scores, -jnp.inf)
        top = jnp.max(scores, axis=0, keepdims=True)
        weights = jnp.exp2(scores - top)
        weights = weights * (1.0 / jnp.sum(weights, axis=0, keepdims=True))
        probs[...] = weights
        low_weights = weights.astype(BF16)
        out = dot(values.T, low_weights, ((1,), (0,))).astype(BF16)
        unstack(att_ref, part, g, out.T)
        att_copy(part, g).start()

        @pl.when(has_grads)
        def _():
            delta = jnp.sum(grad.T.astype(F32) * out.astype(F32), axis=0, keepdims=True)
            weight_grad = dot(values, grad, ((1,), (1,)))
            p = probs[...]
            score_grad = (p * (weight_grad - delta) * scale).astype(BF16)
            query_grad = dot(keys.T, score_grad, ((1,), (0,))).astype(BF16)
            unstack(dq, part, g, query_grad.T)
            dq_copy(part, g).start()
            acc[g, window, :HEAD_SIZE] += dot(score_grad, query, ((1,), (0,)))
            acc[g, window, HEAD_SIZE:] += dot(p.astype(BF16), grad, ((1,), (0,)))

    def pair_copy(g, part, step, owner):
        at = (g, part, step)
        return remote(
            dkv.at[g, block_rows(block_of(owner, part))], pair.at[at],
            pair_send.at[at], pair_recv.at[at], "ctx", partner,
        )

    def sum_copy(g, part, step, owner):
        at = (g, part, step)
        return remote(
            paired.at[at], recv.at[at], sum_send.at[at], sum_recv.at[at], "ctx", owner
        )

    def terms_to_partner(g, act):
        for step in (*range(1, pairs), 0):
            for part in range(2):
                owner = ahead(step) * 2 + 1 - side

                @pl.when(used(me, owner, part))
                def _():
                    act(pair_copy(g, part, step, owner))

    def start_terms(g):
        @pl.when(has_grads)
        def _():
            dkv[g] = acc[g].astype(BF16)
            terms_to_partner(g, lambda copy: copy.start())

    def own_and_pair(g, part, step, owner):
        @pl.when(used(partner, owner, part))
        def _():
            pair_copy(g, part, step, owner).wait_recv()

        return dkv[g, block_rows(block_of(owner, part)), :].astype(F32) + pair[
            g, part, step
        ].astype(F32)

    def sums_along_line(g):
        @pl.when(has_grads)
        def _():
            for step in range(1, pairs):
                for part in range(2):
                    owner = ahead(step) * 2 + side

                    @pl.when(used_by_pair(line, owner, part))
                    def _():
                        paired[g, part, step] = own_and_pair(g, part, step, owner).astype(BF16)
                        sum_copy(g, part, step, owner).start()

    def finish(g):
        @pl.when(has_grads)
        def _():
            for part in range(2):
                total = own_and_pair(g, part, 0, me)
                for step in range(1, pairs):
                    @pl.when(used_by_pair(behind(step), me, part))
                    def _():
                        sum_copy(g, part, step, behind(step) * 2 + side).wait_recv()

                    total = total + recv[g, part, step].astype(F32)
                total = total.astype(BF16)
                fin[g, 0, part * half:(part + 1) * half, :] = total[:, :HEAD_SIZE]
                fin[g, 1, part * half:(part + 1) * half, :] = total[:, HEAD_SIZE:]
            for index in range(2):
                fin_copy(g, index).start()

    pass_keys(0)
    send_keys(1, lambda copy: copy.start())
    wait_passed(0)
    unit(1, 0)
    pass_keys(1)
    unit(0, 0)
    start_terms(0)
    wait_passed(1)
    unit(1, 1)
    sums_along_line(0)
    unit(0, 1)
    start_terms(1)
    finish(0)
    sums_along_line(1)
    finish(1)

    for part in range(2):
        for g in range(KEY_VALUE_HEADS):
            att_copy(part, g).wait()

    @pl.when(jnp.logical_not(has_next))
    def _():
        for fill in fills:
            fill.wait()

    for g in range(KEY_VALUE_HEADS):
        send_keys(g, lambda copy: copy.wait_send())
        wait_pass_sent(g)

    @pl.when(has_grads)
    def _():
        for g in range(KEY_VALUE_HEADS):
            terms_to_partner(g, lambda copy: copy.wait_send())
            for part in range(2):
                for step in range(1, pairs):
                    owner = ahead(step) * 2 + side

                    @pl.when(used_by_pair(line, owner, part))
                    def _():
                        sum_copy(g, part, step, owner).wait_send()

                dq_copy(part, g).wait_send()
                fin_copy(g, part).wait_send()

    @pl.when(has_next)
    def _():
        for g in range(KEY_VALUE_HEADS):
            for part in range(2):
                dq_copy(part, g).wait_recv()
                fin_copy(g, part).wait_recv()


def write_out(*refs):
    size = (len(refs) - 2) // 3
    sources, targets, held = (refs[k * size:(k + 1) * size] for k in range(3))
    load_sem, store_sem = refs[-2:]
    loads = [
        pltpu.make_async_copy(sources[i], held[i], load_sem.at[i]) for i in range(size)
    ]
    stores = [
        pltpu.make_async_copy(held[i], targets[i], store_sem.at[i]) for i in range(size)
    ]
    for load in loads:
        load.start()
    for load, store in zip(loads, stores):
        load.wait()
        store.start()
    for store in stores:
        store.wait()


def solution(mesh):
    count, sections = mesh.shape["ctx"], mesh.shape["pipe"]

    def local(queries, keys, values, out_grad, doc_blocks):
        rows, columns = queries.shape[1:]
        half = rows // 2
        span = count * half
        heads = columns // HEAD_SIZE
        group = heads // KEY_VALUE_HEADS
        pairs = count // 2
        hbm = pl.BlockSpec(memory_space=pltpu.HBM)
        dma = pltpu.SemaphoreType.DMA
        outputs = tuple(
            jax.ShapeDtypeStruct(x.shape, BF16) for x in (queries, queries, keys, values)
        )
        blocks = (KEY_VALUE_HEADS, 2, pairs)
        terms = (KEY_VALUE_HEADS, 2 * span, 2 * HEAD_SIZE)
        results = pl.pallas_call(
            functools.partial(kernel, count, sections, heads, doc_blocks.shape[1]),
            out_shape=outputs,
            in_specs=[hbm] * 5,
            out_specs=(hbm,) * 4,
            scratch_shapes=[
                pltpu.VMEM(queries.shape, BF16),
                pltpu.VMEM(queries.shape, BF16),
                pltpu.SMEM(doc_blocks.shape, jnp.int32),
                pltpu.VMEM(queries.shape, BF16),
                pltpu.VMEM(queries.shape, BF16),
                pltpu.VMEM(keys.shape, BF16),
                pltpu.VMEM(keys.shape, BF16),
                pltpu.VMEM(terms, BF16),
                pltpu.VMEM(terms, F32),
                pltpu.VMEM(terms, BF16),
                pltpu.VMEM((*blocks, half, 2 * HEAD_SIZE), BF16),
                pltpu.VMEM((*blocks, half, 2 * HEAD_SIZE), BF16),
                pltpu.VMEM((*blocks, half, 2 * HEAD_SIZE), BF16),
                pltpu.VMEM((span, group * half), F32),
                pltpu.VMEM(queries.shape, BF16),
                pltpu.VMEM((KEY_VALUE_HEADS, 2, rows, HEAD_SIZE), BF16),
                dma((5,)),
                dma((2 * KEY_VALUE_HEADS + 3,)),
                *[dma(blocks)] * 8,
                *[dma((2 * KEY_VALUE_HEADS,))] * 2,
                *[dma((KEY_VALUE_HEADS, 2))] * 2,
            ],
            compiler_params=pltpu.CompilerParams(
                collective_id=0, has_side_effects=True, vmem_limit_bytes=VMEM_BYTES
            ),
        )(doc_blocks, queries, keys, values, out_grad)
        return pl.pallas_call(
            write_out,
            out_shape=outputs,
            in_specs=[hbm] * 4,
            out_specs=(hbm,) * 4,
            scratch_shapes=[pltpu.VMEM(x.shape, BF16) for x in outputs] + [dma((4,))] * 2,
            compiler_params=pltpu.CompilerParams(vmem_limit_bytes=VMEM_BYTES),
        )(*results)

    split = P(("dp", "pipe"), "ctx", None)
    return jax.shard_map(
        local,
        mesh=mesh,
        in_specs=(split, split, split, split, P(("dp", "pipe"), None)),
        out_specs=(split,) * 4,
        check_vma=False,
    )
```
